128 devices in a mesh: acq: 16 (over z_hi, x, core), az: 8 (over z_lo, y).
Axes of the slice: x: 4, y: 4, z: 4 (z_hi: 2, z_lo: 2; z = z_hi * 2 + z_lo), core: 2. Of those that a mesh axis runs over, the one named last changes fastest.
Arguments:
- slc: float32 [64, 2, 320, 2560], P('acq', None, 'az'), may hold values from -12 to 12
- ref_ids: int32 [4], replicated, may hold values from 0 to 63, as said below
- partners: int32 [4, 8], replicated, may hold values from 0 to 63, as said below
- offsets: int32 [4, 8], replicated, may hold values from -4 to 4, as said below
- fracs: int32 [4, 8], replicated, may hold values from 0 to 63
Outputs:
- coherence: float32 [4, 64, 2, 64, 128], P(None, 'acq', None, 'az')
The draws below stay inside these ranges and needn't reach their ends.
Inputs may be any that keep to these rules, and one draw needn't show every extreme that they name: `ref_ids`: acquisitions that are references; the reference of a step is never among that step's partners. `partners`: each row names 8 different acquisitions; no block of 4 consecutive acquisitions that one index of acq holds contains more than 2 of one row, and in every row some block contains exactly 2. `offsets`: both ends of the range occur in every draw.
All inputs are finite; a program needn't handle non-finite values.
Results may differ from the reference program's by a relative error of at most 0.0001.
Values sent between devices are 32-bit elements; how exact they have to be, the bound alone decides.
A program may use at most 128 MiB of HBM per device.

```python
import jax
import jax.numpy as jnp
from jax import lax

ACQ_DEV = 4
RG = 2560
STEPS = 4
PARTNERS = 8
PAIR_DEV = 2
TAPS = 8
NFRAC = 64
MAXOFF = 4
LOOK_AZ = 5
LOOK_RG = 20
ACQ = 64
AZ = 320


def place_local(local_perm, owner_dev, target_local):
    row = local_perm[owner_dev]
    current = row[PAIR_DEV]
    row = jnp.where(row == target_local, current, row)
    row = row.at[PAIR_DEV].set(target_local)
    return local_perm.at[owner_dev].set(row.astype(jnp.int32))


def pair_plan(key):
    base_key = jax.random.fold_in(key, 7001)
    device_count = ACQ // ACQ_DEV
    ref_list = []
    partner_list = []
    for step_index in range(STEPS):
        step_key = jax.random.fold_in(base_key, step_index)
        order_key, cand_key, local_key, owner_key = jax.random.split(step_key, 4)
        devices_order = jax.random.permutation(order_key, device_count).astype(jnp.int32)
        full_dev = devices_order[0]
        other_devs = devices_order[1:]
        candidates = jax.random.permutation(cand_key, (device_count - 1) * PAIR_DEV).astype(jnp.int32)
        picked = candidates[:PARTNERS - PAIR_DEV]
        other_dev = other_devs[picked // PAIR_DEV]
        other_slot = picked % PAIR_DEV
        dev_of = jnp.concatenate([jnp.full((PAIR_DEV,), full_dev, jnp.int32), other_dev])
        slot_of = jnp.concatenate([jnp.arange(PAIR_DEV, dtype=jnp.int32), other_slot])
        local_perm = jax.vmap(lambda subkey: jax.random.permutation(subkey, ACQ_DEV).astype(jnp.int32))(jax.random.split(local_key, device_count))
        owner_dev = jax.random.randint(owner_key, (), 0, device_count).astype(jnp.int32)
        if step_index == 0:
            owner_dev = jnp.asarray(device_count - 1, jnp.int32)
            local_perm = place_local(local_perm, owner_dev, ACQ_DEV - 1)
        elif step_index == 1:
            owner_dev = jnp.asarray(0, jnp.int32)
            local_perm = place_local(local_perm, owner_dev, 0)
        partner_row = dev_of * ACQ_DEV + local_perm[dev_of, slot_of]
        ref_list.append(owner_dev * ACQ_DEV + local_perm[owner_dev, PAIR_DEV])
        partner_list.append(partner_row)
    return (jnp.stack(ref_list).astype(jnp.int32), jnp.stack(partner_list).astype(jnp.int32))


def draw_ref_ids(key, part):
    return pair_plan(key)[0]


def draw_partners(key, part):
    return pair_plan(key)[1]


def draw_offsets(key, part):
    value_key, place_key = jax.random.split(jax.random.fold_in(key, 3301))
    values = jax.random.randint(value_key, (STEPS * PARTNERS,), -MAXOFF, MAXOFF + 1).astype(jnp.int32)
    places = jax.random.permutation(place_key, STEPS * PARTNERS).astype(jnp.int32)
    values = values.at[places[0]].set(MAXOFF)
    values = values.at[places[1]].set(-MAXOFF)
    return values.reshape(STEPS, PARTNERS)


def draw_slc(key, part):
    scene_key, speckle_key = jax.random.split(jax.random.fold_in(key, 11), 2)
    white_noise = jax.random.normal(scene_key, (2, AZ + 7, RG), jnp.float32)
    scene_part = white_noise[:, 0:AZ]
    for tap_lag in range(1, 8):
        scene_part = scene_part + white_noise[:, tap_lag:tap_lag + AZ]
    scene_part = scene_part / jnp.sqrt(8.0)
    speckle = jax.random.normal(speckle_key, (ACQ, 2, AZ, RG), jnp.float32)
    plane = 0.8 * scene_part[None] + 0.6 * speckle
    return jnp.clip(plane, -12.0, 12.0)


def place_ends(values, own_key, smallest, largest):
    extent = values.shape
    place = [jax.random.randint(jax.random.fold_in(own_key, axis), (), 0, extent[axis]) for axis in range(len(extent))]
    values = values.at[tuple(place)].set(smallest)
    longest = extent.index(max(extent))
    place[longest] = (place[longest] + 1) % extent[longest]
    return values.at[tuple(place)].set(largest)


def setup_inputs(seed: int = 0) -> dict:
    keys = jax.random.split(jax.random.key(seed), 6)
    return {
        "slc": draw_slc(jax.random.fold_in(keys[5], 71), 0),
        "ref_ids": draw_ref_ids(jax.random.fold_in(keys[5], 71), 0),
        "partners": draw_partners(jax.random.fold_in(keys[5], 71), 0),
        "offsets": draw_offsets(jax.random.fold_in(keys[5], 71), 0),
        "fracs": place_ends(jax.random.randint(keys[4], (STEPS, PARTNERS), 0, NFRAC), jax.random.fold_in(keys[4], 1), 0, NFRAC - 1).astype(jnp.int32),
    }


def sinc_taps(frac_index):
    fraction = frac_index.astype(jnp.float32) / NFRAC
    tap_place = jnp.arange(TAPS, dtype=jnp.float32) - 3.0
    distance = tap_place - fraction
    return jnp.sinc(distance) * (0.5 + 0.5 * jnp.cos(jnp.pi * distance / 4.0))

def resample(padded, shift_rows, weights, tile_rows):
    margin = MAXOFF + 4
    start_row = (margin + shift_rows - 3).astype(jnp.int32)
    window = lax.dynamic_slice_in_dim(padded, start_row, tile_rows + TAPS - 1, axis=1)
    resampled = weights[0] * window[:, 0:tile_rows]
    for tap_index in range(1, TAPS):
        resampled = resampled + weights[tap_index] * window[:, tap_index:tap_index + tile_rows]
    return resampled

def multilook(plane):
    leading = plane.shape[:-2]
    line_count, range_cols = plane.shape[-2:]
    shaped = plane.reshape(leading + (line_count // LOOK_AZ, LOOK_AZ, range_cols // LOOK_RG, LOOK_RG))
    return shaped.sum(axis=(-3, -1))

def coherence_of(ref_tile, sec_tile):
    ref_re, ref_im = (ref_tile[0], ref_tile[1])
    sec_re, sec_im = (sec_tile[0], sec_tile[1])
    cross_re = multilook(ref_re * sec_re + ref_im * sec_im)
    cross_im = multilook(ref_im * sec_re - ref_re * sec_im)
    power_ref = multilook(ref_re * ref_re + ref_im * ref_im)
    power_sec = multilook(sec_re * sec_re + sec_im * sec_im)
    scaling = lax.rsqrt(power_ref * power_sec + 1e-06)
    return jnp.stack([cross_re * scaling, cross_im * scaling])

def reference(slc, ref_ids, partners, offsets, fracs):
    margin = MAXOFF + 4
    result = jnp.zeros((STEPS, ACQ, 2, AZ // LOOK_AZ, RG // LOOK_RG), jnp.float32)
    for step_index in range(STEPS):
        ref_tile = slc[ref_ids[step_index]]
        for slot_index in range(PARTNERS):
            partner_id = partners[step_index, slot_index]
            padded = jnp.pad(slc[partner_id], ((0, 0), (margin, margin), (0, 0)))
            weights = sinc_taps(fracs[step_index, slot_index])
            resampled = resample(padded, offsets[step_index, slot_index], weights, AZ)
            result = result.at[step_index, partner_id].set(coherence_of(ref_tile, resampled))
    return result
```

```python
from functools import partial

import jax
import jax.numpy as jnp
import numpy as np
from jax import lax
from jax.experimental import pallas as pl
from jax.experimental.pallas import tpu as pltpu
from jax.sharding import PartitionSpec as P

STEPS = 4
PARTNERS = 8
HELD = 4
TAPS = 8
NFRAC = 64
ROWS = 40
HALO = 8
LOOK_AZ = 5
LOOK_RG = 20
RG = 2560
LANES = 128
COLS = RG // LANES
LOOKS = RG // LOOK_RG
XS = 4
GROUP = COLS // XS
CHUNK = 208
HALF = CHUNK // 2
CUTS = ((0, 56), (56, 48))
WAVES = len(CUTS)
MESH = pl.DeviceIdType.MESH
DEPTH = 256


def tap_table():
    distance = np.arange(TAPS)[None, :] - 3.0 - np.arange(NFRAC)[:, None] / NFRAC
    table = np.sinc(distance) * (0.5 + 0.5 * np.cos(np.pi * distance / 4.0))
    return table.astype(np.float32).reshape(-1)


def kernel(
    slots,
    ref_ids,
    partners,
    offsets,
    fracs,
    table,
    slc,
    out,
    tile,
    padded,
    mate_send,
    mate_recv,
    slot_data,
    got0,
    got1,
    refs,
    moved,
    cross,
    power,
    look,
    local_sem,
    fill_sem,
    own_sem,
    mate_sem,
    halo_sem,
    rs_sem,
    ag_sem,
    core_sem,
):
    got = (got0, got1)
    acq = lax.axis_index("acq")
    az = lax.axis_index("az")
    az_count = lax.axis_size("az")
    zh = acq // 8
    x = (acq // 2) % XS
    core = acq % 2
    chip = acq // 2

    def device(zz, xx, cc):
        return (zz * 8 + (xx % XS) * 2 + cc, az)

    mate = device(zh, x, 1 - core)
    right = device(zh, x + 1, core)
    left = device(zh, x + 3, core)
    across = device(1 - zh, x, core)
    peers = [(dz, dx) for dz in range(2) for dx in range(XS) if (dz, dx) != (0, 0)]

    loads = []
    for ct in range(COLS):
        copy = pltpu.make_async_copy(
            slc.at[:, :, :, pl.ds(ct * LANES, LANES)], tile.at[:, :, ct], local_sem.at[ct]
        )
        copy.start()
        loads.append(copy)

    barrier = pltpu.get_barrier_semaphore()
    pl.semaphore_signal(barrier, inc=1, device_id=mate, device_id_type=MESH)
    for dz, dx in peers:
        pl.semaphore_signal(
            barrier,
            inc=1,
            device_id=device((zh + dz) % 2, x + dx, core),
            device_id_type=MESH,
        )

    @pl.when(az > 0)
    def _():
        pl.semaphore_signal(barrier, inc=1, device_id=(acq, az - 1), device_id_type=MESH)

    @pl.when(az < az_count - 1)
    def _():
        pl.semaphore_signal(barrier, inc=1, device_id=(acq, az + 1), device_id_type=MESH)

    owner, rank = [], []
    slot_image = [jnp.int32(0)] * slots
    slot_core = [jnp.int32(0)] * slots
    for s in range(STEPS):
        ref = ref_ids[s]
        chip_of = lax.div(ref, jnp.int32(8))
        core_of = lax.rem(lax.div(ref, jnp.int32(4)), jnp.int32(2))
        image = lax.rem(ref, jnp.int32(4))
        place = jnp.int32(0)
        for other in owner:
            place = place + jnp.where(other == chip_of, 1, 0).astype(jnp.int32)
        owner.append(chip_of)
        rank.append(place)
        for j in range(slots):
            mine = jnp.logical_and(chip_of == chip, place == j)
            slot_image[j] = jnp.where(mine, image, slot_image[j])
            slot_core[j] = jnp.where(mine, core_of, slot_core[j])

    for copy in loads:
        copy.wait()

    pad = jnp.zeros((CHUNK - GROUP * ROWS, LANES), jnp.float32)
    for j in range(slots):

        @pl.loop(0, XS)
        def _(xx):
            for ctl in range(GROUP):
                mate_send[j, xx, pl.ds(ctl * ROWS, ROWS), :] = tile[
                    slot_image[j], 1 - core, xx * GROUP + ctl
                ]
            mate_send[j, xx, pl.ds(GROUP * ROWS, CHUNK - GROUP * ROWS), :] = pad

    fill = pltpu.make_async_copy(tile, padded.at[:, :, :, pl.ds(HALO, ROWS), :], fill_sem)
    fill.start()

    pl.semaphore_wait(
        barrier,
        1 + len(peers) + jnp.where(az > 0, 1, 0) + jnp.where(az < az_count - 1, 1, 0),
    )

    swap = pltpu.make_async_remote_copy(
        mate_send, mate_recv, mate_sem.at[0], mate_sem.at[1], device_id=mate, device_id_type=MESH
    )
    swap.start()

    up = pltpu.make_async_remote_copy(
        tile.at[:, :, :, pl.ds(ROWS - HALO, HALO), :],
        padded.at[:, :, :, pl.ds(0, HALO), :],
        halo_sem.at[0],
        halo_sem.at[1],
        device_id=(acq, az + 1),
        device_id_type=MESH,
    )
    down = pltpu.make_async_remote_copy(
        tile.at[:, :, :, pl.ds(0, HALO), :],
        padded.at[:, :, :, pl.ds(ROWS + HALO, HALO), :],
        halo_sem.at[2],
        halo_sem.at[3],
        device_id=(acq, az - 1),
        device_id_type=MESH,
    )

    @pl.when(az < az_count - 1)
    def _():
        up.start()

    @pl.when(az > 0)
    def _():
        down.start()

    def clear(first):
        @pl.loop(0, HELD * 2 * COLS)
        def _(i):
            padded[i // (2 * COLS), (i // COLS) % 2, i % COLS, pl.ds(first, HALO), :] = jnp.zeros(
                (HALO, LANES), jnp.float32
            )

    @pl.when(az == 0)
    def _():
        clear(0)

    @pl.when(az == az_count - 1)
    def _():
        clear(ROWS + HALO)

    swap.wait_recv()
    for j in range(slots):
        keep = slot_core[j] == core

        @pl.loop(0, XS)
        def _(xx):
            for ctl in range(GROUP):
                rows = pl.ds(ctl * ROWS, ROWS)
                slot_data[j, xx, rows, :] = jnp.where(
                    keep, tile[slot_image[j], core, xx * GROUP + ctl], mate_recv[j, xx, rows, :]
                )
            slot_data[j, xx, pl.ds(GROUP * ROWS, CHUNK - GROUP * ROWS), :] = pad

    scatter = []
    for w, (first, count) in enumerate(CUTS):
        copies = []
        for i, (dz, dx) in enumerate(peers):
            zz = (zh + dz) % 2
            xx = (x + dx) % XS
            copy = pltpu.make_async_remote_copy(
                slot_data.at[:, xx, pl.ds(pl.multiple_of(zz * HALF + first, 8), count), :],
                got[w].at[chip],
                rs_sem.at[0, w, i],
                rs_sem.at[1, w, i],
                device_id=device(zz, xx, core),
                device_id_type=MESH,
            )
            copy.start()
            copies.append(copy)
        keep_own = pltpu.make_async_copy(
            slot_data.at[:, x, pl.ds(pl.multiple_of(zh * HALF + first, 8), count), :],
            got[w].at[chip],
            own_sem.at[w],
        )
        keep_own.start()
        scatter.append((copies, keep_own))

    column = lax.broadcasted_iota(jnp.int32, (DEPTH, LOOKS), 0)
    block = lax.broadcasted_iota(jnp.int32, (DEPTH, LOOKS), 1) * LOOK_RG

    @pl.loop(0, RG // DEPTH)
    def _(i):
        offset = column + i * DEPTH - block
        look[pl.ds(pl.multiple_of(i * DEPTH, DEPTH), DEPTH), :] = jnp.where(
            jnp.logical_and(offset >= 0, offset < LOOK_RG), 1.0, 0.0
        ).astype(jnp.bfloat16)

    pairs = []
    for s in range(STEPS):
        found = jnp.int32(0)
        chosen = [[jnp.int32(0), jnp.int32(0), jnp.int32(0), jnp.int32(-1)] for _ in range(2)]
        for p in range(PARTNERS):
            partner = partners[s, p]
            here = lax.div(partner, jnp.int32(HELD)) == acq
            image = lax.rem(partner, jnp.int32(HELD))
            for i in range(2):
                take = jnp.logical_and(here, found == i)
                chosen[i] = [
                    jnp.where(take, image, chosen[i][0]),
                    jnp.where(take, offsets[s, p], chosen[i][1]),
                    jnp.where(take, fracs[s, p], chosen[i][2]),
                    jnp.where(take, image, chosen[i][3]),
                ]
            found = found + jnp.where(here, 1, 0).astype(jnp.int32)
        pairs.append(chosen)

    sent = []

    def where_at(zz, xx, w, steps=(0, STEPS)):
        first, count = CUTS[w]
        return refs.at[
            pl.ds(steps[0], steps[1]),
            core,
            xx % XS,
            pl.ds(pl.multiple_of(zz * HALF + first, 8), count),
            :,
        ]

    def send(place, sems, index, target):
        copy = pltpu.make_async_remote_copy(
            place,
            place,
            sems.at[(0,) + index],
            sems.at[(1,) + index],
            device_id=target,
            device_id_type=MESH,
        )
        copy.start()
        sent.append(copy)
        return copy

    to_mate = []
    shared = [0] * WAVES

    def share(place, w):
        to_mate.append(send(place, core_sem, (w, shared[w]), mate))
        shared[w] += 1

    events = []
    for w, (first, count) in enumerate(CUTS):
        copies, keep_own = scatter[w]
        for copy in copies:
            copy.wait_recv()
        keep_own.wait()
        for s in range(STEPS):
            refs[s, core, x, pl.ds(pl.multiple_of(zh * HALF + first, 8), count), :] = got[w][
                owner[s], rank[s]
            ]
        mine = where_at(zh, x, w)
        events.append(
            [
                send(mine, ag_sem, (w, 0), right),
                send(mine, ag_sem, (w, 1), left),
                send(mine, ag_sem, (w, 2), across),
            ]
        )
        share(mine, w)

    for w in range(WAVES):
        ev = events[w]
        ev[0].wait_recv()
        ev.append(send(where_at(zh, x + 3, w, (0, 2)), ag_sem, (w, 3), right))
        ev[1].wait_recv()
        ev.append(send(where_at(zh, x + 1, w, (2, 2)), ag_sem, (w, 4), left))
        ev[2].wait_recv()
        ev.append(send(where_at(1 - zh, x, w), ag_sem, (w, 5), right))
        ev.append(send(where_at(1 - zh, x, w), ag_sem, (w, 6), left))
        share(where_at(zh, x + 3, w), w)
        share(where_at(zh, x + 1, w), w)
        share(where_at(1 - zh, x, w), w)

    fill.wait()

    @pl.when(az > 0)
    def _():
        up.wait_recv()

    @pl.when(az < az_count - 1)
    def _():
        down.wait_recv()

    def resample(s):
        for i in range(2):
            image, shift, frac, _ = pairs[s][i]
            weights = [table[frac * TAPS + t] for t in range(TAPS)]
            base = HALO - 3 + shift

            @pl.loop(0, COLS)
            def _(ct):
                total = jnp.zeros((8, LANES), jnp.float32)
                for part in range(2):
                    lines = [
                        padded[image, part, ct, pl.ds(base + m, 8, stride=LOOK_AZ), :]
                        for m in range(LOOK_AZ + TAPS - 1)
                    ]
                    for j in range(LOOK_AZ):
                        value = weights[0] * lines[j]
                        for t in range(1, TAPS):
                            value = value + weights[t] * lines[j + t]
                        moved[s * 2 + i, part, ct, j] = value
                        total = total + value * value
                power[
                    (s * 2 + i) * 8 : (s * 2 + i) * 8 + 8,
                    pl.ds(pl.multiple_of(ct * LANES, LANES), LANES),
                ] = total

    resample(0)
    for w in range(WAVES):
        ev = events[w]
        ev[3].wait_recv()
        ev[4].wait_recv()
        ev.append(send(where_at(zh, x + 2, w), ag_sem, (w, 7), across))
        share(where_at(zh, x + 2, w), w)
        resample(1 + w)

    resample(3)
    for w in range(WAVES):
        ev = events[w]
        ev[5].wait_recv()
        share(where_at(1 - zh, x + 3, w), w)
        ev[6].wait_recv()
        share(where_at(1 - zh, x + 1, w), w)
    for w in range(WAVES):
        events[w][7].wait_recv()
        share(where_at(1 - zh, x + 2, w), w)
    for copy in to_mate:
        copy.wait_recv()

    def products(s):
        @pl.loop(0, XS)
        def _(xx):
            for ctl in range(GROUP):
                ct = xx * GROUP + ctl
                cols = pl.ds(pl.multiple_of(ct * LANES, LANES), LANES)
                sums = [jnp.zeros((8, LANES), jnp.float32) for _ in range(5)]
                for j in range(LOOK_AZ):
                    rows = pl.ds(ctl * ROWS + j, 8, stride=LOOK_AZ)
                    re = refs[s, 0, xx, rows, :]
                    im = refs[s, 1, xx, rows, :]
                    sums[4] = sums[4] + (re * re + im * im)
                    for i in range(2):
                        sre = moved[s * 2 + i, 0, ct, j]
                        sim = moved[s * 2 + i, 1, ct, j]
                        sums[2 * i] = sums[2 * i] + (re * sre + im * sim)
                        sums[2 * i + 1] = sums[2 * i + 1] + (im * sre - re * sim)
                for k in range(5):
                    cross[s * 40 + k * 8 : s * 40 + k * 8 + 8, cols] = sums[k]

    for s in range(STEPS):
        products(s)

    def boxed(planes, count):
        def step(i, total):
            rows = pl.ds(pl.multiple_of(i * DEPTH, DEPTH), DEPTH)
            value = planes[:, rows]
            high = value.astype(jnp.bfloat16)
            low = (value - high.astype(jnp.float32)).astype(jnp.bfloat16)
            weights = look[rows, :]
            total = total + jnp.dot(high, weights, preferred_element_type=jnp.float32)
            return total + jnp.dot(low, weights, preferred_element_type=jnp.float32)

        return lax.fori_loop(0, RG // DEPTH, step, jnp.zeros((count, LOOKS), jnp.float32))

    powers = boxed(power, STEPS * 2 * 8)
    crosses = boxed(cross, STEPS * 40)
    for s in range(STEPS):
        plane = [crosses[s * 40 + k * 8 : s * 40 + k * 8 + 8] for k in range(5)]
        results = []
        for i in range(2):
            sec = powers[(s * 2 + i) * 8 : (s * 2 + i) * 8 + 8]
            scaling = lax.rsqrt(plane[4] * sec + 1e-06)
            results.append([plane[2 * i] * scaling, plane[2 * i + 1] * scaling])
        for a in range(HELD):
            for c in range(2):
                value = jnp.where(pairs[s][1][3] == a, results[1][c], 0.0)
                out[s, a, c] = jnp.where(pairs[s][0][3] == a, results[0][c], value)

    swap.wait_send()
    for copies, _ in scatter:
        for copy in copies:
            copy.wait_send()
    for copy in sent:
        copy.wait_send()

    @pl.when(az < az_count - 1)
    def _():
        up.wait_send()

    @pl.when(az > 0)
    def _():
        down.wait_send()


def body(slc, ref_ids, partners, offsets, fracs, slots=4):
    dma = pltpu.SemaphoreType.DMA
    smem = pl.BlockSpec(memory_space=pltpu.SMEM)
    f32 = jnp.float32
    return pl.pallas_call(
        partial(kernel, slots),
        out_shape=jax.ShapeDtypeStruct((STEPS, HELD, 2, ROWS // LOOK_AZ, LOOKS), f32),
        in_specs=[smem] * 5 + [pl.BlockSpec(memory_space=pl.ANY)],
        out_specs=pl.BlockSpec(memory_space=pltpu.VMEM),
        scratch_shapes=[
            pltpu.VMEM((HELD, 2, COLS, ROWS, LANES), f32),
            pltpu.VMEM((HELD, 2, COLS, ROWS + 2 * HALO, LANES), f32),
            pltpu.VMEM((slots, XS, CHUNK, LANES), f32),
            pltpu.VMEM((slots, XS, CHUNK, LANES), f32),
            pltpu.VMEM((slots, XS, CHUNK, LANES), f32),
            pltpu.VMEM((8, slots, CUTS[0][1], LANES), f32),
            pltpu.VMEM((8, slots, CUTS[1][1], LANES), f32),
            pltpu.VMEM((STEPS, 2, XS, CHUNK, LANES), f32),
            pltpu.VMEM((STEPS * 2, 2, COLS, LOOK_AZ, 8, LANES), f32),
            pltpu.VMEM((STEPS * 40, RG), f32),
            pltpu.VMEM((STEPS * 2 * 8, RG), f32),
            pltpu.VMEM((RG, LOOKS), jnp.bfloat16),
            dma((COLS,)),
            dma,
            dma((WAVES,)),
            dma((2,)),
            dma((4,)),
            dma((2, WAVES, 7)),
            dma((2, WAVES, 8)),
            dma((2, WAVES, 8)),
        ],
        compiler_params=pltpu.CompilerParams(
            collective_id=0, has_side_effects=True, vmem_limit_bytes=52 * 2**20
        ),
    )(ref_ids, partners, offsets, fracs, jnp.asarray(tap_table()), slc)


def solution(mesh):
    in_specs = (P("acq", None, "az", None), P(), P(), P(), P())
    out_specs = P(None, "acq", None, "az", None)
    return jax.shard_map(body, mesh=mesh, in_specs=in_specs, out_specs=out_specs, check_vma=False)
```

```python
from functools import partial

import jax
import jax.numpy as jnp
import numpy as np
from jax import lax
from jax.experimental import pallas as pl
from jax.experimental.pallas import tpu as pltpu
from jax.sharding import PartitionSpec as P

STEPS = 4
PARTNERS = 8
HELD = 4
TAPS = 8
NFRAC = 64
ROWS = 40
HALO = 8
LOOK_AZ = 5
LOOK_RG = 20
RG = 2560
LANES = 128
COLS = RG // LANES
LOOKS = RG // LOOK_RG
XS = 4
GROUP = COLS // XS
CUTS = ((0, 1), (1, 1), (2, 1), (3, 1), (4, 1))
WAVES = len(CUTS)
MESH = pl.DeviceIdType.MESH


def tap_table():
    distance = np.arange(TAPS)[None, :] - 3.0 - np.arange(NFRAC)[:, None] / NFRAC
    table = np.sinc(distance) * (0.5 + 0.5 * np.cos(np.pi * distance / 4.0))
    return table.astype(np.float32).reshape(-1)


def kernel(
    slots,
    ref_hbm,
    partners_hbm,
    offsets_hbm,
    fracs_hbm,
    table_hbm,
    slc,
    out,
    ref_ids,
    partners,
    offsets,
    fracs,
    table,
    tile,
    padded,
    mate_send,
    mate_recv,
    slot_data,
    candidate,
    other_half,
    refs,
    moved,
    cross,
    power,
    look,
    small_sem,
    local_sem,
    fill_sem,
    own_sem,
    mate_sem,
    halo_sem,
    rs_sem,
    z_sem,
    ag_sem,
    core_sem,
    *got,
):
    acq = lax.axis_index("acq")
    az = lax.axis_index("az")
    az_count = lax.axis_size("az")
    zh = acq // 8
    x = (acq // 2) % XS
    core = acq % 2
    chip = acq // 2

    def device(zz, xx, cc):
        return (zz * 8 + (xx % XS) * 2 + cc, az)

    mate = device(zh, x, 1 - core)
    right = device(zh, x + 1, core)
    left = device(zh, x + 3, core)
    across = device(1 - zh, x, core)

    smalls = []
    for i, (a, b) in enumerate(
        [
            (ref_hbm, ref_ids),
            (partners_hbm, partners),
            (offsets_hbm, offsets),
            (fracs_hbm, fracs),
            (table_hbm, table),
        ]
    ):
        copy = pltpu.make_async_copy(a, b, small_sem.at[i])
        copy.start()
        smalls.append(copy)

    loads = []
    for w, (first, count) in enumerate(CUTS):
        copies = []
        for c in range(first, first + count):
            for xx in range(XS):
                ct = xx * GROUP + c
                copy = pltpu.make_async_copy(
                    slc.at[:, :, :, pl.ds(ct * LANES, LANES)], tile.at[:, :, ct], local_sem.at[ct]
                )
                copy.start()
                copies.append(copy)
        loads.append(copies)

    barrier = pltpu.get_barrier_semaphore()
    neighbours = [mate, right, left, device(zh, x + 2, core), across]
    for other in neighbours:
        pl.semaphore_signal(barrier, inc=1, device_id=other, device_id_type=MESH)

    @pl.when(az > 0)
    def _():
        pl.semaphore_signal(barrier, inc=1, device_id=(acq, az - 1), device_id_type=MESH)

    @pl.when(az < az_count - 1)
    def _():
        pl.semaphore_signal(barrier, inc=1, device_id=(acq, az + 1), device_id_type=MESH)

    for copy in smalls:
        copy.wait()
    owner, rank = [], []
    slot_image = [jnp.int32(0)] * slots
    slot_core = [jnp.int32(0)] * slots
    for s in range(STEPS):
        ref = ref_ids[s]
        chip_of = lax.div(ref, jnp.int32(8))
        core_of = lax.rem(lax.div(ref, jnp.int32(4)), jnp.int32(2))
        image = lax.rem(ref, jnp.int32(4))
        place = jnp.int32(0)
        for earlier in owner:
            place = place + jnp.where(earlier == chip_of, 1, 0).astype(jnp.int32)
        owner.append(chip_of)
        rank.append(place)
        for j in range(slots):
            mine = jnp.logical_and(chip_of == chip, place == j)
            slot_image[j] = jnp.where(mine, image, slot_image[j])
            slot_core[j] = jnp.where(mine, core_of, slot_core[j])

    for copies in loads:
        for copy in copies:
            copy.wait()

    def remote(source, target, sems, index, place):
        copy = pltpu.make_async_remote_copy(
            source,
            target,
            sems.at[(0,) + index],
            sems.at[(1,) + index],
            device_id=place,
            device_id_type=MESH,
        )
        copy.start()
        return copy

    swaps = []
    for w, (first, count) in enumerate(CUTS):

        @pl.loop(0, XS)
        def _(xx):
            for c in range(first, first + count):
                for j in range(slots):
                    ct = xx * GROUP + c
                    mate_send[w, j, xx * count + c - first] = tile[slot_image[j], 1 - core, ct]

        if w == 0:
            pl.semaphore_wait(
                barrier,
                len(neighbours)
                + jnp.where(az > 0, 1, 0)
                + jnp.where(az < az_count - 1, 1, 0),
            )
        cells = pl.ds(0, XS * count)
        swaps.append(
            remote(mate_send.at[w, :, cells], mate_recv.at[w, :, cells], mate_sem, (w,), mate)
        )

    up = pltpu.make_async_remote_copy(
        tile.at[:, :, :, pl.ds(ROWS - HALO, HALO), :],
        padded.at[:, :, :, pl.ds(0, HALO), :],
        halo_sem.at[0],
        halo_sem.at[1],
        device_id=(acq, az + 1),
        device_id_type=MESH,
    )
    down = pltpu.make_async_remote_copy(
        tile.at[:, :, :, pl.ds(0, HALO), :],
        padded.at[:, :, :, pl.ds(ROWS + HALO, HALO), :],
        halo_sem.at[2],
        halo_sem.at[3],
        device_id=(acq, az - 1),
        device_id_type=MESH,
    )

    @pl.when(az < az_count - 1)
    def _():
        up.start()

    @pl.when(az > 0)
    def _():
        down.start()

    scatter = []
    for w, (first, count) in enumerate(CUTS):
        swaps[w].wait_recv()

        @pl.loop(0, XS)
        def _(xx):
            for c in range(first, first + count):
                for j in range(slots):
                    ct = xx * GROUP + c
                    slot_data[w, j, xx * count + c - first] = jnp.where(
                        slot_core[j] == core,
                        tile[slot_image[j], core, ct],
                        mate_recv[w, j, xx * count + c - first],
                    )

        copies = []
        for i in range(1, XS):
            xx = (x + i) % XS
            copies.append(
                remote(
                    slot_data.at[w, :, pl.ds(xx * count, count)],
                    got[w].at[x],
                    rs_sem,
                    (w, i - 1),
                    device(zh, xx, core),
                )
            )
        keep_own = pltpu.make_async_copy(
            slot_data.at[w, :, pl.ds(x * count, count)], got[w].at[x], own_sem.at[w]
        )
        keep_own.start()
        scatter.append((copies, keep_own))

    fill = pltpu.make_async_copy(tile, padded.at[:, :, :, pl.ds(HALO, ROWS), :], fill_sem)
    fill.start()

    def clear(first):
        @pl.loop(0, HELD * 2 * COLS)
        def _(i):
            padded[i // (2 * COLS), (i // COLS) % 2, i % COLS, pl.ds(first, HALO), :] = jnp.zeros(
                (HALO, LANES), jnp.float32
            )

    @pl.when(az == 0)
    def _():
        clear(0)

    @pl.when(az == az_count - 1)
    def _():
        clear(ROWS + HALO)

    lane = lax.broadcasted_iota(jnp.int32, (LANES, LOOKS), 0)
    block = lax.broadcasted_iota(jnp.int32, (LANES, LOOKS), 1) * LOOK_RG
    starts = []
    for w, (first, count) in enumerate(CUTS):
        starts.append(first * XS * LANES)

        @pl.loop(0, XS)
        def _(xx):
            for c in range(first, first + count):
                offset = lane + (xx * GROUP + c) * LANES - block
                row = first * XS * LANES + (xx * count + c - first) * LANES
                look[pl.ds(pl.multiple_of(row, LANES), LANES), :] = jnp.where(
                    jnp.logical_and(offset >= 0, offset < LOOK_RG), 1.0, 0.0
                ).astype(jnp.bfloat16)

    pairs = []
    for s in range(STEPS):
        found = jnp.int32(0)
        chosen = [[jnp.int32(0), jnp.int32(0), jnp.int32(0), jnp.int32(-1)] for _ in range(2)]
        for p in range(PARTNERS):
            partner = partners[s, p]
            here = lax.div(partner, jnp.int32(HELD)) == acq
            image = lax.rem(partner, jnp.int32(HELD))
            for i in range(2):
                take = jnp.logical_and(here, found == i)
                chosen[i] = [
                    jnp.where(take, image, chosen[i][0]),
                    jnp.where(take, offsets[s, p], chosen[i][1]),
                    jnp.where(take, fracs[s, p], chosen[i][2]),
                    jnp.where(take, image, chosen[i][3]),
                ]
            found = found + jnp.where(here, 1, 0).astype(jnp.int32)
        pairs.append(chosen)

    waiting = []

    def where_at(xx, w, first_step=0, steps=STEPS):
        first, count = CUTS[w]
        return refs.at[pl.ds(first_step, steps), core, pl.ds((xx % XS) * GROUP + first, count)]

    def pass_on(place, index, target):
        copy = remote(place, place, ag_sem, index, target)
        waiting.append(copy)
        return copy

    shares = [[] for _ in CUTS]

    def share(place, w):
        shares[w].append(remote(place, place, core_sem, (w, len(shares[w])), mate))

    across_copies = [None] * WAVES
    gathers = [None] * WAVES
    relays = [None] * WAVES

    def dealt(w):
        copies, keep_own = scatter[w]
        for copy in copies:
            copy.wait_recv()
        keep_own.wait()
        for s in range(STEPS):
            for c in range(CUTS[w][1]):
                candidate[w, s, c] = got[w][lax.rem(owner[s], jnp.int32(XS)), rank[s], c]
        cells = pl.ds(0, CUTS[w][1])
        across_copies[w] = remote(
            candidate.at[w, :, cells], other_half.at[w, :, cells], z_sem, (w,), across
        )

    def gather(w):
        first, count = CUTS[w]
        across_copies[w].wait_recv()
        for s in range(STEPS):
            near = lax.div(owner[s], jnp.int32(XS)) == zh
            for c in range(count):
                refs[s, core, x * GROUP + first + c] = jnp.where(
                    near, candidate[w, s, c], other_half[w, s, c]
                )
        gathers[w] = [
            pass_on(where_at(x, w), (w, 0), right),
            pass_on(where_at(x, w), (w, 1), left),
        ]
        share(where_at(x, w), w)

    def relay(w):
        gathers[w][0].wait_recv()
        first = pass_on(where_at(x + 3, w, 0, 2), (w, 2), right)
        gathers[w][1].wait_recv()
        relays[w] = [first, pass_on(where_at(x + 1, w, 2, 2), (w, 3), left)]
        share(where_at(x + 3, w), w)
        share(where_at(x + 1, w), w)

    def last(w):
        relays[w][0].wait_recv()
        relays[w][1].wait_recv()
        share(where_at(x + 2, w), w)

    def halos():
        fill.wait()

        @pl.when(az > 0)
        def _():
            up.wait_recv()

        @pl.when(az < az_count - 1)
        def _():
            down.wait_recv()

    def resample(s):
        for i in range(2):
            image, shift, frac, _ = pairs[s][i]
            weights = [table[frac * TAPS + t] for t in range(TAPS)]
            base = HALO - 3 + shift
            rows = pl.ds((s * 2 + i) * 8, 8)
            for first, count in CUTS:

                @pl.loop(0, XS)
                def _(xx):
                    for c in range(count):
                        ct = xx * GROUP + first + c
                        total = jnp.zeros((8, LANES), jnp.float32)
                        for part in range(2):
                            lines = [
                                padded[image, part, ct, pl.ds(base + m, 8, stride=LOOK_AZ), :]
                                for m in range(LOOK_AZ + TAPS - 1)
                            ]
                            for j in range(LOOK_AZ):
                                value = weights[0] * lines[j]
                                for t in range(1, TAPS):
                                    value = value + weights[t] * lines[j + t]
                                moved[s * 2 + i, part, ct, j] = value
                                total = total + value * value
                        place = (first * XS + xx * count + c) * LANES
                        power[rows, pl.ds(pl.multiple_of(place, LANES), LANES)] = total

    def products(w):
        first, count = CUTS[w]
        for s in range(STEPS):

            @pl.loop(0, XS)
            def _(xx):
                for c in range(count):
                    ct = xx * GROUP + first + c
                    sums = [jnp.zeros((8, LANES), jnp.float32) for _ in range(5)]
                    for j in range(LOOK_AZ):
                        lines = pl.ds(j, 8, stride=LOOK_AZ)
                        re = refs[s, 0, ct, lines, :]
                        im = refs[s, 1, ct, lines, :]
                        sums[4] = sums[4] + (re * re + im * im)
                        for i in range(2):
                            sre = moved[s * 2 + i, 0, ct, j]
                            sim = moved[s * 2 + i, 1, ct, j]
                            sums[2 * i] = sums[2 * i] + (re * sre + im * sim)
                            sums[2 * i + 1] = sums[2 * i + 1] + (im * sre - re * sim)
                    place = (first * XS + xx * count + c) * LANES
                    cols = pl.ds(pl.multiple_of(place, LANES), LANES)
                    for k in range(5):
                        cross[s * 40 + k * 8 : s * 40 + k * 8 + 8, cols] = sums[k]

    def boxed(planes, begin, size):
        value = planes[:, begin : begin + size]
        high = value.astype(jnp.bfloat16)
        low = (value - high.astype(jnp.float32)).astype(jnp.bfloat16)
        weights = look[begin : begin + size, :]
        total = jnp.dot(high, weights, preferred_element_type=jnp.float32)
        return total + jnp.dot(low, weights, preferred_element_type=jnp.float32)

    crosses = None
    for name, w in ORDER:
        if name == "dealt":
            dealt(w)
        elif name == "gather":
            gather(w)
        elif name == "relay":
            relay(w)
        elif name == "last":
            last(w)
        elif name == "halos":
            halos()
        elif name == "resample":
            resample(w)
        elif name == "powers":
            powers = boxed(power, 0, RG)
        else:
            for copy in shares[w]:
                copy.wait_recv()
            products(w)
            part = boxed(cross, starts[w], CUTS[w][1] * XS * LANES)
            crosses = part if crosses is None else crosses + part

    for s in range(STEPS):
        plane = [crosses[s * 40 + k * 8 : s * 40 + k * 8 + 8] for k in range(5)]
        results = []
        for i in range(2):
            sec = powers[(s * 2 + i) * 8 : (s * 2 + i) * 8 + 8]
            scaling = lax.rsqrt(plane[4] * sec + 1e-06)
            results.append([plane[2 * i] * scaling, plane[2 * i + 1] * scaling])
        for a in range(HELD):
            for c in range(2):
                value = jnp.where(pairs[s][1][3] == a, results[1][c], 0.0)
                out[s, a, c] = jnp.where(pairs[s][0][3] == a, results[0][c], value)

    for copy in swaps + across_copies + waiting:
        copy.wait_send()
    for copies, _ in scatter:
        for copy in copies:
            copy.wait_send()
    for copies in shares:
        for copy in copies:
            copy.wait_send()

    @pl.when(az < az_count - 1)
    def _():
        up.wait_send()

    @pl.when(az > 0)
    def _():
        down.wait_send()


ORDER = (
    [("dealt", 0), ("dealt", 1), ("dealt", 2), ("gather", 0), ("dealt", 3), ("gather", 1)]
    + [("dealt", 4), ("gather", 2), ("relay", 0), ("gather", 3), ("relay", 1), ("gather", 4)]
    + [("halos", 0), ("resample", 0), ("last", 0), ("relay", 2), ("resample", 1), ("last", 1)]
    + [("relay", 3), ("resample", 2), ("last", 2), ("relay", 4), ("resample", 3), ("powers", 0)]
    + [("last", 3), ("products", 0), ("products", 1), ("last", 4), ("products", 2)]
    + [("products", 3), ("products", 4)]
)


def body(slc, ref_ids, partners, offsets, fracs, slots=4):
    dma = pltpu.SemaphoreType.DMA
    anywhere = pl.BlockSpec(memory_space=pl.ANY)
    f32 = jnp.float32
    widest = max(count for _, count in CUTS)
    return pl.pallas_call(
        partial(kernel, slots),
        out_shape=jax.ShapeDtypeStruct((STEPS, HELD, 2, ROWS // LOOK_AZ, LOOKS), f32),
        in_specs=[anywhere] * 6,
        out_specs=pl.BlockSpec(memory_space=pltpu.VMEM),
        scratch_shapes=[
            pltpu.SMEM((STEPS,), jnp.int32),
            pltpu.SMEM((STEPS, PARTNERS), jnp.int32),
            pltpu.SMEM((STEPS, PARTNERS), jnp.int32),
            pltpu.SMEM((STEPS, PARTNERS), jnp.int32),
            pltpu.SMEM((NFRAC * TAPS,), f32),
            pltpu.VMEM((HELD, 2, COLS, ROWS, LANES), f32),
            pltpu.VMEM((HELD, 2, COLS, ROWS + 2 * HALO, LANES), f32),
            pltpu.VMEM((WAVES, slots, XS * widest, ROWS, LANES), f32),
            pltpu.VMEM((WAVES, slots, XS * widest, ROWS, LANES), f32),
            pltpu.VMEM((WAVES, slots, XS * widest, ROWS, LANES), f32),
            pltpu.VMEM((WAVES, STEPS, widest, ROWS, LANES), f32),
            pltpu.VMEM((WAVES, STEPS, widest, ROWS, LANES), f32),
            pltpu.VMEM((STEPS, 2, COLS, ROWS, LANES), f32),
            pltpu.VMEM((STEPS * 2, 2, COLS, LOOK_AZ, 8, LANES), f32),
            pltpu.VMEM((STEPS * 40, RG), f32),
            pltpu.VMEM((STEPS * 2 * 8, RG), f32),
            pltpu.VMEM((RG, LOOKS), jnp.bfloat16),
            dma((5,)),
            dma((COLS,)),
            dma,
            dma((WAVES,)),
            dma((2, WAVES)),
            dma((4,)),
            dma((2, WAVES, XS - 1)),
            dma((2, WAVES)),
            dma((2, WAVES, 4)),
            dma((2, WAVES, 4)),
        ]
        + [pltpu.VMEM((XS, slots, count, ROWS, LANES), f32) for _, count in CUTS],
        compiler_params=pltpu.CompilerParams(
            collective_id=0, has_side_effects=True, vmem_limit_bytes=52 * 2**20
        ),
    )(ref_ids, partners, offsets, fracs, jnp.asarray(tap_table()), slc)


def solution(mesh):
    in_specs = (P("acq", None, "az", None), P(), P(), P(), P())
    out_specs = P(None, "acq", None, "az", None)
    return jax.shard_map(body, mesh=mesh, in_specs=in_specs, out_specs=out_specs, check_vma=False)
```

```python
from functools import partial

import jax
import jax.numpy as jnp
import numpy as np
from jax import lax
from jax.experimental import pallas as pl
from jax.experimental.pallas import tpu as pltpu
from jax.sharding import PartitionSpec as P

STEPS = 4
PARTNERS = 8
HELD = 4
TAPS = 8
NFRAC = 64
ROWS = 40
HALO = 8
LOOK_AZ = 5
LOOK_RG = 20
RG = 2560
LANES = 128
COLS = RG // LANES
LOOKS = RG // LOOK_RG
XS = 4
GROUP = COLS // XS
CUTS = ((0, 1), (1, 1), (2, 1), (3, 1), (4, 1))
WAVES = len(CUTS)
DETOURS = (1, 3)
MESH = pl.DeviceIdType.MESH


def tap_table():
    distance = np.arange(TAPS)[None, :] - 3.0 - np.arange(NFRAC)[:, None] / NFRAC
    table = np.sinc(distance) * (0.5 + 0.5 * np.cos(np.pi * distance / 4.0))
    return table.astype(np.float32).reshape(-1)


def kernel(
    slots,
    ref_hbm,
    partners_hbm,
    offsets_hbm,
    fracs_hbm,
    table_hbm,
    slc,
    out,
    ref_ids,
    partners,
    offsets,
    fracs,
    table,
    tile,
    mate_send,
    mate_recv,
    slot_data,
    candidate,
    other_half,
    refs,
    moved,
    cross,
    power,
    look,
    passing,
    small_sem,
    local_sem,
    fill_sem,
    own_sem,
    mate_sem,
    halo_sem,
    passing_sem,
    rs_sem,
    z_sem,
    ag_sem,
    core_sem,
    *per_wave,
):
    got, padded = per_wave[:WAVES], per_wave[WAVES:]
    acq = lax.axis_index("acq")
    az = lax.axis_index("az")
    az_count = lax.axis_size("az")
    zh = acq // 8
    x = (acq // 2) % XS
    core = acq % 2
    chip = acq // 2

    def device(zz, xx, cc):
        return (zz * 8 + (xx % XS) * 2 + cc, az)

    mate = device(zh, x, 1 - core)
    right = device(zh, x + 1, core)
    left = device(zh, x + 3, core)
    across = device(1 - zh, x, core)

    smalls = []
    for i, (a, b) in enumerate(
        [
            (ref_hbm, ref_ids),
            (partners_hbm, partners),
            (offsets_hbm, offsets),
            (fracs_hbm, fracs),
            (table_hbm, table),
        ]
    ):
        copy = pltpu.make_async_copy(a, b, small_sem.at[i])
        copy.start()
        smalls.append(copy)

    loads = []
    for w, (first, count) in enumerate(CUTS):
        copies = []
        for c in range(first, first + count):
            for xx in range(XS):
                ct = xx * GROUP + c
                copy = pltpu.make_async_copy(
                    slc.at[:, :, :, pl.ds(ct * LANES, LANES)],
                    tile.at[:, :, c * XS + xx],
                    local_sem.at[ct],
                )
                copy.start()
                copies.append(copy)
        loads.append(copies)

    barrier = pltpu.get_barrier_semaphore()
    neighbours = [mate, right, left, device(zh, x + 2, core), across]
    for other in neighbours:
        pl.semaphore_signal(barrier, inc=1, device_id=other, device_id_type=MESH)

    @pl.when(az > 0)
    def _():
        pl.semaphore_signal(barrier, inc=1, device_id=(acq, az - 1), device_id_type=MESH)

    @pl.when(az < az_count - 1)
    def _():
        pl.semaphore_signal(barrier, inc=1, device_id=(acq, az + 1), device_id_type=MESH)

    run = az_count // 2
    leaves_up = az == run - 1
    leaves_down = az == run
    passes_up = az == az_count - 1
    passes_down = az == 0
    edge = az % run
    is_edge = jnp.logical_or(edge == 0, edge == run - 1)
    opposite = (az + run) % az_count
    helped = jnp.where(az < run, jnp.where(az == 0, run - 1, 0), jnp.where(az == run, az_count - 1, run))

    @pl.when(is_edge)
    def _():
        for other in (opposite, helped):
            pl.semaphore_signal(barrier, inc=1, device_id=(acq, other), device_id_type=MESH)

    for copy in smalls:
        copy.wait()
    owner, rank = [], []
    slot_image = [jnp.int32(0)] * slots
    slot_core = [jnp.int32(0)] * slots
    for s in range(STEPS):
        ref = ref_ids[s]
        chip_of = lax.div(ref, jnp.int32(8))
        core_of = lax.rem(lax.div(ref, jnp.int32(4)), jnp.int32(2))
        image = lax.rem(ref, jnp.int32(4))
        place = jnp.int32(0)
        for earlier in owner:
            place = place + jnp.where(earlier == chip_of, 1, 0).astype(jnp.int32)
        owner.append(chip_of)
        rank.append(jnp.minimum(place, slots - 1))
        for j in range(slots):
            mine = jnp.logical_and(chip_of == chip, place == j)
            slot_image[j] = jnp.where(mine, image, slot_image[j])
            slot_core[j] = jnp.where(mine, core_of, slot_core[j])

    def remote(source, target, sems, index, place):
        copy = pltpu.make_async_remote_copy(
            source,
            target,
            sems.at[(0,) + index],
            sems.at[(1,) + index],
            device_id=place,
            device_id_type=MESH,
        )
        copy.start()
        return copy

    for copies in loads:
        for copy in copies:
            copy.wait()
    for w, (first, count) in enumerate(CUTS):

        @pl.loop(0, XS)
        def _(xx):
            for c in range(first, first + count):
                for j in range(slots):
                    place = c * XS + xx
                    mate_send[w, j, xx * count + c - first] = tile[slot_image[j], 1 - core, place]

    pl.semaphore_wait(
        barrier,
        len(neighbours)
        + jnp.where(az > 0, 1, 0)
        + jnp.where(az < az_count - 1, 1, 0)
        + jnp.where(is_edge, 2, 0),
    )

    low_rows, tail_rows = pl.ds(0, HALO), pl.ds(ROWS - HALO, HALO)
    high_rows = pl.ds(ROWS + HALO, HALO)

    def halo(source, target, index, w, place):
        return pltpu.make_async_remote_copy(
            source,
            target,
            halo_sem.at[0, index, w],
            halo_sem.at[1, index, w],
            device_id=(acq, place),
            device_id_type=MESH,
        )

    def detour(rows, n, places):
        return pltpu.make_async_remote_copy(
            tile.at[:, :, places, rows, :],
            passing.at[n, :, :, pl.ds(0, places.size)],
            passing_sem.at[0, n],
            passing_sem.at[1, n],
            device_id=(acq, opposite),
            device_id_type=MESH,
        )

    has_up, has_down = az < az_count - 1, az > 0
    straight_up = jnp.logical_and(has_up, jnp.logical_not(leaves_up))
    straight_down = jnp.logical_and(has_down, jnp.logical_not(leaves_down))
    up, down, inner, crossing, onwards, detours = [], [], [], [], [], {}
    for w, (first, count) in enumerate(CUTS):
        places = pl.ds(first * XS, count * XS)
        up_place = padded[w].at[:, :, :, low_rows, :]
        down_place = padded[w].at[:, :, :, high_rows, :]
        up.append(halo(tile.at[:, :, places, tail_rows, :], up_place, 0, w, az + 1))
        down.append(halo(tile.at[:, :, places, low_rows, :], down_place, 1, w, az - 1))
        if w in DETOURS:
            n = DETOURS.index(w)
            source = passing.at[n, :, :, pl.ds(0, count * XS)]
            detour_up, detour_down = detour(tail_rows, n, places), detour(low_rows, n, places)
            crossing.append([(leaves_up, detour_up), (leaves_down, detour_down)])
            detours[w] = (
                detour_up,
                (passes_up, halo(source, up_place, 0, w, run)),
                (passes_down, halo(source, down_place, 1, w, run - 1)),
            )
            onwards += detours[w][1:]
        else:
            crossing.append([(leaves_up, up[w]), (leaves_down, down[w])])
        inner += [(straight_up, up[w]), (straight_down, down[w])]

    def cross_over(w):
        for condition, copy in crossing[w]:
            pl.when(condition)(copy.start)

    for w in EARLY:
        cross_over(w)
    for condition, copy in inner:
        pl.when(condition)(copy.start)

    swaps = []
    for w, (first, count) in enumerate(CUTS):
        cells = pl.ds(0, XS * count)
        swaps.append(
            remote(mate_send.at[w, :, cells], mate_recv.at[w, :, cells], mate_sem, (w,), mate)
        )

    scatter = []
    for w, (first, count) in enumerate(CUTS):
        swaps[w].wait_recv()

        @pl.loop(0, XS)
        def _(xx):
            for c in range(first, first + count):
                for j in range(slots):
                    place = c * XS + xx
                    slot_data[w, j, xx * count + c - first] = jnp.where(
                        slot_core[j] == core,
                        tile[slot_image[j], core, place],
                        mate_recv[w, j, xx * count + c - first],
                    )

        copies = []
        for i in range(1, XS):
            xx = (x + i) % XS
            copies.append(
                remote(
                    slot_data.at[w, :, pl.ds(xx * count, count)],
                    got[w].at[x],
                    rs_sem,
                    (w, i - 1),
                    device(zh, xx, core),
                )
            )
        keep_own = pltpu.make_async_copy(
            slot_data.at[w, :, pl.ds(x * count, count)], got[w].at[x], own_sem.at[w]
        )
        keep_own.start()
        scatter.append((copies, keep_own))

    fills = []
    for w, (first, count) in enumerate(CUTS):
        fill = pltpu.make_async_copy(
            tile.at[:, :, pl.ds(first * XS, count * XS)],
            padded[w].at[:, :, :, pl.ds(HALO, ROWS), :],
            fill_sem.at[w],
        )
        fill.start()
        fills.append(fill)

    def clear(start):
        for w, (first, count) in enumerate(CUTS):

            @pl.loop(0, HELD * 2)
            def _(i):
                for n in range(count * XS):
                    padded[w][i // 2, i % 2, n, pl.ds(start, HALO), :] = jnp.zeros(
                        (HALO, LANES), jnp.float32
                    )

    @pl.when(az == 0)
    def _():
        clear(0)

    @pl.when(az == az_count - 1)
    def _():
        clear(ROWS + HALO)

    lane = lax.broadcasted_iota(jnp.int32, (LANES, LOOKS), 0)
    block = lax.broadcasted_iota(jnp.int32, (LANES, LOOKS), 1) * LOOK_RG
    starts = []
    for w, (first, count) in enumerate(CUTS):
        starts.append(first * XS * LANES)

        @pl.loop(0, XS)
        def _(xx):
            for c in range(first, first + count):
                offset = lane + (xx * GROUP + c) * LANES - block
                row = first * XS * LANES + (xx * count + c - first) * LANES
                look[pl.ds(pl.multiple_of(row, LANES), LANES), :] = jnp.where(
                    jnp.logical_and(offset >= 0, offset < LOOK_RG), 1.0, 0.0
                ).astype(jnp.bfloat16)

    pairs = []
    for s in range(STEPS):
        found = jnp.int32(0)
        chosen = [[jnp.int32(0), jnp.int32(0), jnp.int32(0), jnp.int32(-1)] for _ in range(2)]
        for p in range(PARTNERS):
            partner = partners[s, p]
            here = lax.div(partner, jnp.int32(HELD)) == acq
            image = lax.rem(partner, jnp.int32(HELD))
            for i in range(2):
                take = jnp.logical_and(here, found == i)
                chosen[i] = [
                    jnp.where(take, image, chosen[i][0]),
                    jnp.where(take, offsets[s, p], chosen[i][1]),
                    jnp.where(take, fracs[s, p], chosen[i][2]),
                    jnp.where(take, image, chosen[i][3]),
                ]
            found = found + jnp.where(here, 1, 0).astype(jnp.int32)
        pairs.append(chosen)

    waiting = []

    def where_at(xx, w, first_step=0, steps=STEPS):
        first, count = CUTS[w]
        return refs.at[pl.ds(first_step, steps), core, pl.ds((xx % XS) * GROUP + first, count)]

    def pass_on(place, index, target):
        copy = remote(place, place, ag_sem, index, target)
        waiting.append(copy)
        return copy

    shares = [[] for _ in CUTS]

    def share(place, w):
        shares[w].append(remote(place, place, core_sem, (w, len(shares[w])), mate))

    across_copies = [None] * WAVES
    gathers = [None] * WAVES
    relays = [None] * WAVES

    def dealt(w):
        copies, keep_own = scatter[w]
        for copy in copies:
            copy.wait_recv()
        keep_own.wait()
        for s in range(STEPS):
            for c in range(CUTS[w][1]):
                candidate[w, s, c] = got[w][lax.rem(owner[s], jnp.int32(XS)), rank[s], c]
        cells = pl.ds(0, CUTS[w][1])
        across_copies[w] = remote(
            candidate.at[w, :, cells], other_half.at[w, :, cells], z_sem, (w,), across
        )

    def gather(w):
        first, count = CUTS[w]
        across_copies[w].wait_recv()
        for s in range(STEPS):
            near = lax.div(owner[s], jnp.int32(XS)) == zh
            for c in range(count):
                refs[s, core, x * GROUP + first + c] = jnp.where(
                    near, candidate[w, s, c], other_half[w, s, c]
                )
        gathers[w] = [
            pass_on(where_at(x, w), (w, 0), right),
            pass_on(where_at(x, w), (w, 1), left),
        ]
        share(where_at(x, w), w)

    def relay(w):
        gathers[w][0].wait_recv()
        first = pass_on(where_at(x + 3, w, 0, 2), (w, 2), right)
        gathers[w][1].wait_recv()
        relays[w] = [first, pass_on(where_at(x + 1, w, 2, 2), (w, 3), left)]
        share(where_at(x + 3, w), w)
        share(where_at(x + 1, w), w)

    def last(w):
        relays[w][0].wait_recv()
        relays[w][1].wait_recv()
        share(where_at(x + 2, w), w)

    def onward(w):
        detour_in, first, second = detours[w]
        pl.when(jnp.logical_or(passes_up, passes_down))(detour_in.wait_recv)
        for condition, copy in (first, second):
            pl.when(condition)(copy.start)

    def resample(w):
        fills[w].wait()
        pl.when(has_down)(up[w].wait_recv)
        pl.when(has_up)(down[w].wait_recv)
        first, count = CUTS[w]
        for n in range(2 * STEPS):
            image, shift, frac, _ = pairs[n // 2][n % 2]
            weights = [table[frac * TAPS + t] for t in range(TAPS)]
            base = HALO - 3 + shift

            @pl.loop(0, XS)
            def _(xx):
                for c in range(count):
                    total = jnp.zeros((8, LANES), jnp.float32)
                    for part in range(2):
                        lines = [
                            padded[w][
                                image, part, c * XS + xx, pl.ds(base + m, 8, stride=LOOK_AZ), :
                            ]
                            for m in range(LOOK_AZ + TAPS - 1)
                        ]
                        for j in range(LOOK_AZ):
                            value = weights[0] * lines[j]
                            for t in range(1, TAPS):
                                value = value + weights[t] * lines[j + t]
                            moved[n, part, xx * GROUP + first + c, j] = value
                            total = total + value * value
                    cols = (first * XS + xx * count + c) * LANES
                    power[pl.ds(n * 8, 8), pl.ds(pl.multiple_of(cols, LANES), LANES)] = total

    def products(w):
        first, count = CUTS[w]
        for s in range(STEPS):

            @pl.loop(0, XS)
            def _(xx):
                for c in range(count):
                    ct = xx * GROUP + first + c
                    sums = [jnp.zeros((8, LANES), jnp.float32) for _ in range(5)]
                    for j in range(LOOK_AZ):
                        lines = pl.ds(j, 8, stride=LOOK_AZ)
                        re = refs[s, 0, ct, lines, :]
                        im = refs[s, 1, ct, lines, :]
                        sums[4] = sums[4] + (re * re + im * im)
                        for i in range(2):
                            sre = moved[s * 2 + i, 0, ct, j]
                            sim = moved[s * 2 + i, 1, ct, j]
                            sums[2 * i] = sums[2 * i] + (re * sre + im * sim)
                            sums[2 * i + 1] = sums[2 * i + 1] + (im * sre - re * sim)
                    place = (first * XS + xx * count + c) * LANES
                    cols = pl.ds(pl.multiple_of(place, LANES), LANES)
                    for k in range(5):
                        cross[s * 40 + k * 8 : s * 40 + k * 8 + 8, cols] = sums[k]

    def boxed(planes, begin, size):
        value = planes[:, begin : begin + size]
        high = value.astype(jnp.bfloat16)
        low = (value - high.astype(jnp.float32)).astype(jnp.bfloat16)
        weights = look[begin : begin + size, :]
        total = jnp.dot(high, weights, preferred_element_type=jnp.float32)
        return total + jnp.dot(low, weights, preferred_element_type=jnp.float32)

    crosses = None
    for name, w in ORDER:
        if name == "dealt":
            dealt(w)
        elif name == "gather":
            gather(w)
        elif name == "relay":
            relay(w)
        elif name == "last":
            last(w)
        elif name == "cross":
            cross_over(w)
        elif name == "onward":
            onward(w)
        elif name == "resample":
            resample(w)
        elif name == "powers":
            powers = boxed(power, 0, RG)
        else:
            for copy in shares[w]:
                copy.wait_recv()
            products(w)
            part = boxed(cross, starts[w], CUTS[w][1] * XS * LANES)
            crosses = part if crosses is None else crosses + part

    for s in range(STEPS):
        plane = [crosses[s * 40 + k * 8 : s * 40 + k * 8 + 8] for k in range(5)]
        results = []
        for i in range(2):
            sec = powers[(s * 2 + i) * 8 : (s * 2 + i) * 8 + 8]
            scaling = lax.rsqrt(plane[4] * sec + 1e-06)
            results.append([plane[2 * i] * scaling, plane[2 * i + 1] * scaling])
        for a in range(HELD):
            for c in range(2):
                value = jnp.where(pairs[s][1][3] == a, results[1][c], 0.0)
                out[s, a, c] = jnp.where(pairs[s][0][3] == a, results[0][c], value)

    for copy in swaps + across_copies + waiting:
        copy.wait_send()
    for copies, _ in scatter:
        for copy in copies:
            copy.wait_send()
    for copies in shares:
        for copy in copies:
            copy.wait_send()

    for condition, copy in inner + sum(crossing, []) + onwards:
        pl.when(condition)(copy.wait_send)


EARLY = (0, 1, 2, 3)
ORDER = [
    (item[:-1], int(item[-1]))
    for item in (
        "dealt0 dealt1 dealt2 gather0",
        "dealt3 gather1 resample0 dealt4",
        "gather2 onward1 gather3 relay0",
        "resample1 gather4 cross4 onward3",
        "relay1 resample2 last0 relay2",
        "last1 resample3 relay3 last2",
        "relay4 resample4 powers0 products0",
        "products1 last3 products2 last4",
        "products3 products4",
    )
    for item in item.split()
]


def run(slots, slc, ref_ids, partners, offsets, fracs):
    dma = pltpu.SemaphoreType.DMA
    anywhere = pl.BlockSpec(memory_space=pltpu.HBM)
    f32 = jnp.float32
    widest = max(count for _, count in CUTS)
    return pl.pallas_call(
        partial(kernel, slots),
        out_shape=jax.ShapeDtypeStruct((STEPS, HELD, 2, ROWS // LOOK_AZ, LOOKS), f32),
        in_specs=[anywhere] * 6,
        out_specs=pl.BlockSpec(memory_space=pltpu.VMEM),
        scratch_shapes=[
            pltpu.SMEM((STEPS,), jnp.int32),
            pltpu.SMEM((STEPS, PARTNERS), jnp.int32),
            pltpu.SMEM((STEPS, PARTNERS), jnp.int32),
            pltpu.SMEM((STEPS, PARTNERS), jnp.int32),
            pltpu.SMEM((NFRAC * TAPS,), f32),
            pltpu.VMEM((HELD, 2, COLS, ROWS, LANES), f32),
            pltpu.VMEM((WAVES, slots, XS * widest, ROWS, LANES), f32),
            pltpu.VMEM((WAVES, slots, XS * widest, ROWS, LANES), f32),
            pltpu.VMEM((WAVES, slots, XS * widest, ROWS, LANES), f32),
            pltpu.VMEM((WAVES, STEPS, widest, ROWS, LANES), f32),
            pltpu.VMEM((WAVES, STEPS, widest, ROWS, LANES), f32),
            pltpu.VMEM((STEPS, 2, COLS, ROWS, LANES), f32),
            pltpu.VMEM((STEPS * 2, 2, COLS, LOOK_AZ, 8, LANES), f32),
            pltpu.VMEM((STEPS * 40, RG), f32),
            pltpu.VMEM((STEPS * 2 * 8, RG), f32),
            pltpu.VMEM((RG, LOOKS), jnp.bfloat16),
            pltpu.VMEM((len(DETOURS), HELD, 2, XS * widest, HALO, LANES), f32),
            dma((5,)),
            dma((COLS,)),
            dma((WAVES,)),
            dma((WAVES,)),
            dma((2, WAVES)),
            dma((2, 2, WAVES)),
            dma((2, len(DETOURS))),
            dma((2, WAVES, XS - 1)),
            dma((2, WAVES)),
            dma((2, WAVES, 4)),
            dma((2, WAVES, 4)),
        ]
        + [pltpu.VMEM((XS, slots, count, ROWS, LANES), f32) for _, count in CUTS]
        + [pltpu.VMEM((HELD, 2, XS * count, ROWS + 2 * HALO, LANES), f32) for _, count in CUTS],
        compiler_params=pltpu.CompilerParams(
            collective_id=slots, has_side_effects=True, vmem_limit_bytes=60 * 2**20
        ),
    )(ref_ids, partners, offsets, fracs, jnp.asarray(tap_table()), slc)


def body(slc, ref_ids, partners, offsets, fracs):
    chips = ref_ids // 8
    most = jnp.max(jnp.sum((chips[:, None] == chips[None, :]).astype(jnp.int32), axis=1))
    return lax.cond(
        most <= 2, partial(run, 2), partial(run, STEPS), slc, ref_ids, partners, offsets, fracs
    )


def solution(mesh):
    in_specs = (P("acq", None, "az", None), P(), P(), P(), P())
    out_specs = P(None, "acq", None, "az", None)
    return jax.shard_map(body, mesh=mesh, in_specs=in_specs, out_specs=out_specs, check_vma=False)
```

```python
from functools import partial

import jax
import jax.numpy as jnp
import numpy as np
from jax import lax
from jax.experimental import pallas as pl
from jax.experimental.pallas import tpu as pltpu
from jax.sharding import PartitionSpec as P

STEPS = 4
PARTNERS = 8
HELD = 4
TAPS = 8
NFRAC = 64
ROWS = 40
HALO = 8
LOOK_AZ = 5
LOOK_RG = 20
RG = 2560
LANES = 128
COLS = RG // LANES
LOOKS = RG // LOOK_RG
XS = 4
GROUP = COLS // XS
CUTS = ((0, 1), (1, 1), (2, 1), (3, 1), (4, 1))
WAVES = len(CUTS)
DETOURS = (1, 3)
MESH = pl.DeviceIdType.MESH


def tap_table():
    distance = np.arange(TAPS)[None, :] - 3.0 - np.arange(NFRAC)[:, None] / NFRAC
    table = np.sinc(distance) * (0.5 + 0.5 * np.cos(np.pi * distance / 4.0))
    return table.astype(np.float32).reshape(-1)


def kernel(
    slots,
    ref_hbm,
    partners_hbm,
    offsets_hbm,
    fracs_hbm,
    table_hbm,
    slc,
    out,
    ref_ids,
    partners,
    offsets,
    fracs,
    table,
    tile,
    mate_send,
    mate_recv,
    slot_data,
    candidate,
    other_half,
    refs,
    moved,
    cross,
    power,
    look,
    passing,
    small_sem,
    local_sem,
    fill_sem,
    own_sem,
    mate_sem,
    halo_sem,
    passing_sem,
    rs_sem,
    z_sem,
    ag_sem,
    core_sem,
    *per_wave,
):
    got, padded = per_wave[:WAVES], per_wave[WAVES:]
    acq = lax.axis_index("acq")
    az = lax.axis_index("az")
    az_count = lax.axis_size("az")
    zh = acq // 8
    x = (acq // 2) % XS
    core = acq % 2
    chip = acq // 2

    def device(zz, xx, cc):
        return (zz * 8 + (xx % XS) * 2 + cc, az)

    mate = device(zh, x, 1 - core)
    right = device(zh, x + 1, core)
    left = device(zh, x + 3, core)
    across = device(1 - zh, x, core)

    smalls = []
    for i, (a, b) in enumerate(
        [
            (ref_hbm, ref_ids),
            (partners_hbm, partners),
            (offsets_hbm, offsets),
            (fracs_hbm, fracs),
            (table_hbm, table),
        ]
    ):
        copy = pltpu.make_async_copy(a, b, small_sem.at[i])
        copy.start()
        smalls.append(copy)

    loads = []
    for w, (first, count) in enumerate(CUTS):
        copies = []
        for c in range(first, first + count):
            for xx in range(XS):
                ct = xx * GROUP + c
                copy = pltpu.make_async_copy(
                    slc.at[:, :, :, pl.ds(ct * LANES, LANES)],
                    tile.at[:, :, c * XS + xx],
                    local_sem.at[ct],
                )
                copy.start()
                copies.append(copy)
        loads.append(copies)

    barrier = pltpu.get_barrier_semaphore()
    neighbours = [mate, right, left, device(zh, x + 2, core), across]
    for other in neighbours:
        pl.semaphore_signal(barrier, inc=1, device_id=other, device_id_type=MESH)

    @pl.when(az > 0)
    def _():
        pl.semaphore_signal(barrier, inc=1, device_id=(acq, az - 1), device_id_type=MESH)

    @pl.when(az < az_count - 1)
    def _():
        pl.semaphore_signal(barrier, inc=1, device_id=(acq, az + 1), device_id_type=MESH)

    run = az_count // 2
    leaves_up = az == run - 1
    leaves_down = az == run
    passes_up = az == az_count - 1
    passes_down = az == 0
    edge = az % run
    is_edge = jnp.logical_or(edge == 0, edge == run - 1)
    opposite = (az + run) % az_count
    helped = jnp.where(az < run, jnp.where(az == 0, run - 1, 0), jnp.where(az == run, az_count - 1, run))

    @pl.when(is_edge)
    def _():
        for other in (opposite, helped):
            pl.semaphore_signal(barrier, inc=1, device_id=(acq, other), device_id_type=MESH)

    for copy in smalls:
        copy.wait()
    owner, rank = [], []
    slot_image = [jnp.int32(0)] * slots
    slot_core = [jnp.int32(0)] * slots
    for s in range(STEPS):
        ref = ref_ids[s]
        chip_of = lax.div(ref, jnp.int32(8))
        core_of = lax.rem(lax.div(ref, jnp.int32(4)), jnp.int32(2))
        image = lax.rem(ref, jnp.int32(4))
        place = jnp.int32(0)
        for earlier in owner:
            place = place + jnp.where(earlier == chip_of, 1, 0).astype(jnp.int32)
        owner.append(chip_of)
        rank.append(jnp.minimum(place, slots - 1))
        for j in range(slots):
            mine = jnp.logical_and(chip_of == chip, place == j)
            slot_image[j] = jnp.where(mine, image, slot_image[j])
            slot_core[j] = jnp.where(mine, core_of, slot_core[j])

    def remote(source, target, sems, index, place):
        copy = pltpu.make_async_remote_copy(
            source,
            target,
            sems.at[(0,) + index],
            sems.at[(1,) + index],
            device_id=place,
            device_id_type=MESH,
        )
        copy.start()
        return copy

    for copies in loads:
        for copy in copies:
            copy.wait()
    for w, (first, count) in enumerate(CUTS):

        @pl.loop(0, XS)
        def _(xx):
            for c in range(first, first + count):
                for j in range(slots):
                    place = c * XS + xx
                    mate_send[w, j, xx * count + c - first] = tile[slot_image[j], 1 - core, place]

    pl.semaphore_wait(
        barrier,
        len(neighbours)
        + jnp.where(az > 0, 1, 0)
        + jnp.where(az < az_count - 1, 1, 0)
        + jnp.where(is_edge, 2, 0),
    )

    low_rows, tail_rows = pl.ds(0, HALO), pl.ds(ROWS - HALO, HALO)
    high_rows = pl.ds(ROWS + HALO, HALO)

    def halo(source, target, index, w, place):
        return pltpu.make_async_remote_copy(
            source,
            target,
            halo_sem.at[0, index, w],
            halo_sem.at[1, index, w],
            device_id=(acq, place),
            device_id_type=MESH,
        )

    def detour(rows, n, places):
        return pltpu.make_async_remote_copy(
            tile.at[:, :, places, rows, :],
            passing.at[n, :, :, pl.ds(0, places.size)],
            passing_sem.at[0, n],
            passing_sem.at[1, n],
            device_id=(acq, opposite),
            device_id_type=MESH,
        )

    has_up, has_down = az < az_count - 1, az > 0
    straight_up = jnp.logical_and(has_up, jnp.logical_not(leaves_up))
    straight_down = jnp.logical_and(has_down, jnp.logical_not(leaves_down))
    up, down, inner, crossing, onwards, detours = [], [], [], [], [], {}
    for w, (first, count) in enumerate(CUTS):
        places = pl.ds(first * XS, count * XS)
        up_place = padded[w].at[:, :, :, low_rows, :]
        down_place = padded[w].at[:, :, :, high_rows, :]
        up.append(halo(tile.at[:, :, places, tail_rows, :], up_place, 0, w, az + 1))
        down.append(halo(tile.at[:, :, places, low_rows, :], down_place, 1, w, az - 1))
        if w in DETOURS:
            n = DETOURS.index(w)
            source = passing.at[n, :, :, pl.ds(0, count * XS)]
            detour_up, detour_down = detour(tail_rows, n, places), detour(low_rows, n, places)
            crossing.append([(leaves_up, detour_up), (leaves_down, detour_down)])
            detours[w] = (
                detour_up,
                (passes_up, halo(source, up_place, 0, w, run)),
                (passes_down, halo(source, down_place, 1, w, run - 1)),
            )
            onwards += detours[w][1:]
        else:
            crossing.append([(leaves_up, up[w]), (leaves_down, down[w])])
        inner += [(straight_up, up[w]), (straight_down, down[w])]

    def cross_over(w):
        for condition, copy in crossing[w]:
            pl.when(condition)(copy.start)

    for w in EARLY:
        cross_over(w)
    for condition, copy in inner:
        pl.when(condition)(copy.start)

    swaps = []
    for w, (first, count) in enumerate(CUTS):
        cells = pl.ds(0, XS * count)
        swaps.append(
            remote(mate_send.at[w, :, cells], mate_recv.at[w, :, cells], mate_sem, (w,), mate)
        )

    scatter = []
    for w, (first, count) in enumerate(CUTS):
        swaps[w].wait_recv()

        @pl.loop(0, XS)
        def _(xx):
            for c in range(first, first + count):
                for j in range(slots):
                    place = c * XS + xx
                    slot_data[w, j, xx * count + c - first] = jnp.where(
                        slot_core[j] == core,
                        tile[slot_image[j], core, place],
                        mate_recv[w, j, xx * count + c - first],
                    )

        copies = []
        for i in range(1, XS):
            xx = (x + i) % XS
            copies.append(
                remote(
                    slot_data.at[w, :, pl.ds(xx * count, count)],
                    got[w].at[x],
                    rs_sem,
                    (w, i - 1),
                    device(zh, xx, core),
                )
            )
        keep_own = pltpu.make_async_copy(
            slot_data.at[w, :, pl.ds(x * count, count)], got[w].at[x], own_sem.at[w]
        )
        keep_own.start()
        scatter.append((copies, keep_own))

    fills = []
    for w, (first, count) in enumerate(CUTS):
        fill = pltpu.make_async_copy(
            tile.at[:, :, pl.ds(first * XS, count * XS)],
            padded[w].at[:, :, :, pl.ds(HALO, ROWS), :],
            fill_sem.at[w],
        )
        fill.start()
        fills.append(fill)

    def clear(start):
        for w, (first, count) in enumerate(CUTS):

            @pl.loop(0, HELD * 2)
            def _(i):
                for n in range(count * XS):
                    padded[w][i // 2, i % 2, n, pl.ds(start, HALO), :] = jnp.zeros(
                        (HALO, LANES), jnp.float32
                    )

    @pl.when(az == 0)
    def _():
        clear(0)

    @pl.when(az == az_count - 1)
    def _():
        clear(ROWS + HALO)

    lane = lax.broadcasted_iota(jnp.int32, (LANES, LOOKS), 0)
    block = lax.broadcasted_iota(jnp.int32, (LANES, LOOKS), 1) * LOOK_RG
    starts = []
    for w, (first, count) in enumerate(CUTS):
        starts.append(first * XS * LANES)

        @pl.loop(0, XS)
        def _(xx):
            for c in range(first, first + count):
                offset = lane + (xx * GROUP + c) * LANES - block
                row = first * XS * LANES + (xx * count + c - first) * LANES
                look[pl.ds(pl.multiple_of(row, LANES), LANES), :] = jnp.where(
                    jnp.logical_and(offset >= 0, offset < LOOK_RG), 1.0, 0.0
                ).astype(jnp.bfloat16)

    pairs = []
    for s in range(STEPS):
        found = jnp.int32(0)
        chosen = [[jnp.int32(0), jnp.int32(0), jnp.int32(0), jnp.int32(-1)] for _ in range(2)]
        for p in range(PARTNERS):
            partner = partners[s, p]
            here = lax.div(partner, jnp.int32(HELD)) == acq
            image = lax.rem(partner, jnp.int32(HELD))
            for i in range(2):
                take = jnp.logical_and(here, found == i)
                chosen[i] = [
                    jnp.where(take, image, chosen[i][0]),
                    jnp.where(take, offsets[s, p], chosen[i][1]),
                    jnp.where(take, fracs[s, p], chosen[i][2]),
                    jnp.where(take, image, chosen[i][3]),
                ]
            found = found + jnp.where(here, 1, 0).astype(jnp.int32)
        pairs.append(chosen)

    waiting = []

    def where_at(xx, w, first_step=0, steps=STEPS):
        first, count = CUTS[w]
        return refs.at[pl.ds(first_step, steps), core, pl.ds((xx % XS) * GROUP + first, count)]

    def pass_on(place, index, target):
        copy = remote(place, place, ag_sem, index, target)
        waiting.append(copy)
        return copy

    shares = [[] for _ in CUTS]

    def share(place, w):
        shares[w].append(remote(place, place, core_sem, (w, len(shares[w])), mate))

    across_copies = [None] * WAVES
    gathers = [None] * WAVES
    relays = [None] * WAVES

    def dealt(w):
        copies, keep_own = scatter[w]
        for copy in copies:
            copy.wait_recv()
        keep_own.wait()
        for s in range(STEPS):
            for c in range(CUTS[w][1]):
                candidate[w, s, c] = got[w][lax.rem(owner[s], jnp.int32(XS)), rank[s], c]
        cells = pl.ds(0, CUTS[w][1])
        across_copies[w] = remote(
            candidate.at[w, :, cells], other_half.at[w, :, cells], z_sem, (w,), across
        )

    def gather(w):
        first, count = CUTS[w]
        across_copies[w].wait_recv()
        for s in range(STEPS):
            near = lax.div(owner[s], jnp.int32(XS)) == zh
            for c in range(count):
                refs[s, core, x * GROUP + first + c] = jnp.where(
                    near, candidate[w, s, c], other_half[w, s, c]
                )
        gathers[w] = [
            pass_on(where_at(x, w), (w, 0), right),
            pass_on(where_at(x, w), (w, 1), left),
        ]
        share(where_at(x, w), w)

    def relay(w):
        gathers[w][0].wait_recv()
        first = pass_on(where_at(x + 3, w, 0, 2), (w, 2), right)
        gathers[w][1].wait_recv()
        relays[w] = [first, pass_on(where_at(x + 1, w, 2, 2), (w, 3), left)]
        share(where_at(x + 3, w), w)
        share(where_at(x + 1, w), w)

    def last(w):
        relays[w][0].wait_recv()
        relays[w][1].wait_recv()
        share(where_at(x + 2, w), w)

    def onward(w):
        detour_in, first, second = detours[w]
        pl.when(jnp.logical_or(passes_up, passes_down))(detour_in.wait_recv)
        for condition, copy in (first, second):
            pl.when(condition)(copy.start)

    def resample(w):
        fills[w].wait()
        pl.when(has_down)(up[w].wait_recv)
        pl.when(has_up)(down[w].wait_recv)
        first, count = CUTS[w]
        for n in range(2 * STEPS):
            image, shift, frac, _ = pairs[n // 2][n % 2]
            weights = [table[frac * TAPS + t] for t in range(TAPS)]
            base = HALO - 3 + shift

            @pl.loop(0, XS)
            def _(xx):
                for c in range(count):
                    total = jnp.zeros((8, LANES), jnp.float32)
                    for part in range(2):
                        lines = [
                            padded[w][
                                image, part, c * XS + xx, pl.ds(base + m, 8, stride=LOOK_AZ), :
                            ]
                            for m in range(LOOK_AZ + TAPS - 1)
                        ]
                        for j in range(LOOK_AZ):
                            value = weights[0] * lines[j]
                            for t in range(1, TAPS):
                                value = value + weights[t] * lines[j + t]
                            moved[n, part, xx * GROUP + first + c, j] = value
                            total = total + value * value
                    cols = (first * XS + xx * count + c) * LANES
                    power[pl.ds(n * 8, 8), pl.ds(pl.multiple_of(cols, LANES), LANES)] = total

    def products(w):
        first, count = CUTS[w]
        for s in range(STEPS):

            @pl.loop(0, XS)
            def _(xx):
                for c in range(count):
                    ct = xx * GROUP + first + c
                    sums = [jnp.zeros((8, LANES), jnp.float32) for _ in range(5)]
                    for j in range(LOOK_AZ):
                        lines = pl.ds(j, 8, stride=LOOK_AZ)
                        re = refs[s, 0, ct, lines, :]
                        im = refs[s, 1, ct, lines, :]
                        sums[4] = sums[4] + (re * re + im * im)
                        for i in range(2):
                            sre = moved[s * 2 + i, 0, ct, j]
                            sim = moved[s * 2 + i, 1, ct, j]
                            sums[2 * i] = sums[2 * i] + (re * sre + im * sim)
                            sums[2 * i + 1] = sums[2 * i + 1] + (im * sre - re * sim)
                    place = (first * XS + xx * count + c) * LANES
                    cols = pl.ds(pl.multiple_of(place, LANES), LANES)
                    for k in range(5):
                        cross[s * 40 + k * 8 : s * 40 + k * 8 + 8, cols] = sums[k]

    def boxed(planes, begin, size):
        value = planes[:, begin : begin + size]
        high = value.astype(jnp.bfloat16)
        low = (value - high.astype(jnp.float32)).astype(jnp.bfloat16)
        weights = look[begin : begin + size, :]
        total = jnp.dot(high, weights, preferred_element_type=jnp.float32)
        return total + jnp.dot(low, weights, preferred_element_type=jnp.float32)

    crosses = None
    for name, w in ORDER:
        if name == "dealt":
            dealt(w)
        elif name == "gather":
            gather(w)
        elif name == "relay":
            relay(w)
        elif name == "last":
            last(w)
        elif name == "cross":
            cross_over(w)
        elif name == "onward":
            onward(w)
        elif name == "resample":
            resample(w)
        elif name == "powers":
            powers = boxed(power, 0, RG)
        else:
            for copy in shares[w]:
                copy.wait_recv()
            products(w)
            part = boxed(cross, starts[w], CUTS[w][1] * XS * LANES)
            crosses = part if crosses is None else crosses + part

    for s in range(STEPS):
        plane = [crosses[s * 40 + k * 8 : s * 40 + k * 8 + 8] for k in range(5)]
        results = []
        for i in range(2):
            sec = powers[(s * 2 + i) * 8 : (s * 2 + i) * 8 + 8]
            scaling = lax.rsqrt(plane[4] * sec + 1e-06)
            results.append([plane[2 * i] * scaling, plane[2 * i + 1] * scaling])
        for a in range(HELD):
            for c in range(2):
                value = jnp.where(pairs[s][1][3] == a, results[1][c], 0.0)
                out[s, a, c] = jnp.where(pairs[s][0][3] == a, results[0][c], value)

    for copy in swaps + across_copies + waiting:
        copy.wait_send()
    for copies, _ in scatter:
        for copy in copies:
            copy.wait_send()
    for copies in shares:
        for copy in copies:
            copy.wait_send()

    for condition, copy in inner + sum(crossing, []) + onwards:
        pl.when(condition)(copy.wait_send)


EARLY = (0, 1, 2, 3)
ORDER = [
    (item[:-1], int(item[-1]))
    for item in (
        "dealt0 dealt1 dealt2 gather0",
        "dealt3 gather1 onward1 dealt4",
        "gather2 gather3 relay0",
        "resample0 resample1 gather4 cross4",
        "onward3",
        "relay1 resample2 last0 relay2",
        "last1 resample3 relay3 last2",
        "relay4 resample4 powers0 products0",
        "products1 last3 products2 last4",
        "products3 products4",
    )
    for item in item.split()
]


def run(slots, slc, ref_ids, partners, offsets, fracs):
    dma = pltpu.SemaphoreType.DMA
    anywhere = pl.BlockSpec(memory_space=pltpu.HBM)
    f32 = jnp.float32
    widest = max(count for _, count in CUTS)
    return pl.pallas_call(
        partial(kernel, slots),
        out_shape=jax.ShapeDtypeStruct((STEPS, HELD, 2, ROWS // LOOK_AZ, LOOKS), f32),
        in_specs=[anywhere] * 6,
        out_specs=pl.BlockSpec(memory_space=pltpu.VMEM),
        scratch_shapes=[
            pltpu.SMEM((STEPS,), jnp.int32),
            pltpu.SMEM((STEPS, PARTNERS), jnp.int32),
            pltpu.SMEM((STEPS, PARTNERS), jnp.int32),
            pltpu.SMEM((STEPS, PARTNERS), jnp.int32),
            pltpu.SMEM((NFRAC * TAPS,), f32),
            pltpu.VMEM((HELD, 2, COLS, ROWS, LANES), f32),
            pltpu.VMEM((WAVES, slots, XS * widest, ROWS, LANES), f32),
            pltpu.VMEM((WAVES, slots, XS * widest, ROWS, LANES), f32),
            pltpu.VMEM((WAVES, slots, XS * widest, ROWS, LANES), f32),
            pltpu.VMEM((WAVES, STEPS, widest, ROWS, LANES), f32),
            pltpu.VMEM((WAVES, STEPS, widest, ROWS, LANES), f32),
            pltpu.VMEM((STEPS, 2, COLS, ROWS, LANES), f32),
            pltpu.VMEM((STEPS * 2, 2, COLS, LOOK_AZ, 8, LANES), f32),
            pltpu.VMEM((STEPS * 40, RG), f32),
            pltpu.VMEM((STEPS * 2 * 8, RG), f32),
            pltpu.VMEM((RG, LOOKS), jnp.bfloat16),
            pltpu.VMEM((len(DETOURS), HELD, 2, XS * widest, HALO, LANES), f32),
            dma((5,)),
            dma((COLS,)),
            dma((WAVES,)),
            dma((WAVES,)),
            dma((2, WAVES)),
            dma((2, 2, WAVES)),
            dma((2, len(DETOURS))),
            dma((2, WAVES, XS - 1)),
            dma((2, WAVES)),
            dma((2, WAVES, 4)),
            dma((2, WAVES, 4)),
        ]
        + [pltpu.VMEM((XS, slots, count, ROWS, LANES), f32) for _, count in CUTS]
        + [pltpu.VMEM((HELD, 2, XS * count, ROWS + 2 * HALO, LANES), f32) for _, count in CUTS],
        compiler_params=pltpu.CompilerParams(
            collective_id=slots, has_side_effects=True, vmem_limit_bytes=60 * 2**20
        ),
    )(ref_ids, partners, offsets, fracs, jnp.asarray(tap_table()), slc)


def body(slc, ref_ids, partners, offsets, fracs):
    chips = ref_ids // 8
    most = jnp.max(jnp.sum((chips[:, None] == chips[None, :]).astype(jnp.int32), axis=1))
    return lax.cond(
        most <= 2, partial(run, 2), partial(run, STEPS), slc, ref_ids, partners, offsets, fracs
    )


def solution(mesh):
    in_specs = (P("acq", None, "az", None), P(), P(), P(), P())
    out_specs = P(None, "acq", None, "az", None)
    return jax.shard_map(body, mesh=mesh, in_specs=in_specs, out_specs=out_specs, check_vma=False)
```
